32 devices in a mesh: groups: 2 (over y), dp: 4 (over z), tensor: 4 (over x, core).
Axes of the slice: x: 2, y: 2, z: 4, core: 2. Of those that a mesh axis runs over, the one named last changes fastest.
Arguments:
- activations: bfloat16 [3840, 4096], P(('groups', 'dp')), parts along dimension 0, may hold values from -6 to 6
- out_grads: bfloat16 [3840, 14336], P(('groups', 'dp'), 'tensor'), parts along dimension 0, may hold values from -6 to 6
- query_grads: bfloat16 [2, 14336, 4096], P(None, 'tensor', 'dp'), may hold values from -0.00018310547 to 0.00018310547
- seq_lengths: int32 [32], P('groups'), parts along dimension 0, may hold values from 1 to 120, as said below
- seq_shards: int32 [32], P('groups'), parts along dimension 0, may hold values from 0 to 3, as said below
Outputs:
- scores: float32 [2, 32], P(None, 'groups'), parts along dimension 1
The draws below stay inside these ranges and needn't reach their ends.
There are 2 independent parts, one for each index of `groups`. The reference program is written for one: setup_inputs(seed, part) draws one part's arguments, and reference() takes and returns one part's arrays. A program takes and returns all parts, laid end to end along the dimension named above; an argument that names none is the same for every part. Nothing has to cross between parts.
Inputs may be any that keep to these rules, and one draw needn't show every extreme that they name: `seq_shards`: each of the 4 shard numbers holds exactly 4 sequences. `seq_lengths`: the lengths of the sequences on one shard sum to at most 480, and on some shard to exactly 480; a shard's sequences fill its slots from the first, in order of sequence number.
All inputs are finite; a program needn't handle non-finite values.
Results may differ from the reference program's by a relative error of at most 0.0003.
Values may be sent and summed in bfloat16 or wider, within the bound.
No kernel may reach another device: no remote copies, remote signals or barrier semaphores. Data moves between devices by JAX's collectives and lax.ppermute only.
A program may use at most 128 MiB of HBM per device.

```python
import jax
import jax.numpy as jnp
from jax import lax

OUT_DIM = 14336
IN_DIM = 4096
QUERIES = 2
TOK_DEV = 480
MOST_LEN = 120
SHARDS = 4
SEQS = 16
TOKENS = 1920


def shared_layout(key):
    mixing = jax.random.permutation(jax.random.fold_in(key, 101), SEQS)
    shard = (mixing % SHARDS).astype(jnp.int32)
    limits = jax.random.randint(jax.random.fold_in(key, 102), (SHARDS,), MOST_LEN // 2, MOST_LEN + 1)
    fullest = jax.random.randint(jax.random.fold_in(key, 103), (), 0, SHARDS)
    limits = jnp.where(jnp.arange(SHARDS) == fullest, MOST_LEN, limits)
    raw_bits = jax.random.randint(jax.random.fold_in(key, 104), (SEQS,), 0, 1048576)
    length = 1 + raw_bits % limits[shard]
    length = jnp.where(shard == fullest, MOST_LEN, length)
    return (shard, length.astype(jnp.int32))


def draw_seq_lengths(key, part):
    shard, length = shared_layout(key)
    return length


def draw_seq_shards(key, part):
    shard, length = shared_layout(key)
    return shard


def shard_levels(stream_key, shape, cuts, smallest, largest):
    def one(dim, parts):
        heights = jax.random.uniform(jax.random.fold_in(jax.random.fold_in(stream_key, 6), dim), (parts,), jnp.float32, smallest / len(cuts), largest / len(cuts))
        return jnp.repeat(jnp.exp(heights), shape[dim] // parts).reshape((-1,) + (1,) * (len(shape) - dim - 1))

    level = one(*cuts[0])
    for cut in cuts[1:]:
        level = level * one(*cut)
    return level


def bell_draw(stream_key, dims, spread, most, cuts=(), kind=jnp.bfloat16):
    level = shard_levels(stream_key, dims, cuts, -0.22, 0.18) if cuts else 1.0
    values = jax.random.normal(stream_key, dims, jnp.float32) * spread * level
    return jnp.minimum(jnp.maximum(values, -most), most).astype(kind)


def setup_inputs(seed: int = 0, part: int = 0) -> dict:
    arg_keys = jax.random.split(jax.random.key(seed), 6)
    own_keys = jax.random.split(jax.random.fold_in(arg_keys[5], part), 6)
    return {
        "activations": bell_draw(own_keys[0], (TOKENS, IN_DIM), 1.0, 6.0, ((0, 4),)),
        "out_grads": bell_draw(own_keys[1], (TOKENS, OUT_DIM), 1.0, 6.0, ((0, 4), (1, 4))),
        "query_grads": bell_draw(arg_keys[2], (QUERIES, OUT_DIM, IN_DIM), ((OUT_DIM * IN_DIM * MOST_LEN) ** -0.5), 0.00018310547, ((1, 4), (2, 4))),
        "seq_lengths": draw_seq_lengths(jax.random.fold_in(jax.random.fold_in(arg_keys[5], part), 71), part),
        "seq_shards": draw_seq_shards(jax.random.fold_in(jax.random.fold_in(arg_keys[5], part), 71), part),
    }


def membership(seq_lengths, seq_shards, shard_of, slot_of):
    count = seq_lengths.shape[0]
    order = jnp.arange(count, dtype=jnp.int32)
    same = seq_shards[:, None] == seq_shards[None, :]
    earlier = jnp.logical_and(order[None, :] < order[:, None], same)
    offset = jnp.sum(jnp.where(earlier, seq_lengths[None, :], 0), axis=1).astype(jnp.int32)
    ending = offset + seq_lengths
    inside = (seq_shards[:, None] == shard_of[None, :]) & (slot_of[None, :] >= offset[:, None]) & (slot_of[None, :] < ending[:, None])
    return inside.astype(jnp.float32)


def reference(activations, out_grads, query_grads, seq_lengths, seq_shards):
    acts_wide = activations.astype(jnp.float32)
    collected = []
    for number in range(QUERIES):
        weighted = jnp.dot(out_grads, query_grads[number], preferred_element_type=jnp.float32)
        collected.append(jnp.sum(weighted * acts_wide, axis=1))
    per_token = jnp.stack(collected)
    everyone = jnp.arange(TOKENS, dtype=jnp.int32)
    member = membership(seq_lengths, seq_shards, everyone // TOK_DEV, everyone % TOK_DEV)
    return jnp.dot(per_token, member.T, precision=lax.Precision.HIGHEST)
```

```python
import jax
import jax.numpy as jnp
from jax import lax
from jax.experimental import pallas as pl
from jax.experimental.pallas import tpu as pltpu
from jax.sharding import PartitionSpec as P

LANES = 128
SPAN = 256
WIDTH = 512
TILE = 16
STEP = 12
SHORT = 0
GRAIN = 3


def exchanged(value, axis, flip):
    return lax.ppermute(value, axis, [(i, i ^ flip) for i in range(lax.axis_size(axis))])


def summed(value, axis):
    size = lax.axis_size(axis)
    if size & (size - 1):
        return lax.psum(value, axis)
    flip = 1
    while flip < size:
        value = value + exchanged(value, axis, flip)
        flip *= 2
    return value


def gathered_cols(value, axis, marks):
    size = lax.axis_size(axis)
    last = value.ndim - 1
    if size & (size - 1):
        return lax.all_gather(value, axis, axis=last, tiled=True)
    place = lax.axis_index(axis)
    blocks = [value]
    flip, n = size // 2, 0
    while flip:
        blocks[0] = after(blocks[0], marks[min(n, len(marks) - 1)])
        others = jnp.split(exchanged(jnp.concatenate(blocks, last), axis, flip), len(blocks), last)
        low = (place & flip) == 0
        blocks = [
            jnp.where(low == first, mine, other)
            for mine, other in zip(blocks, others)
            for first in (True, False)
        ]
        flip, n = flip // 2, n + 1
    return jnp.concatenate(blocks, last)


def inside(begin, length, valid, count):
    slot = jnp.arange(count, dtype=jnp.int32)[None, :]
    held = valid[:, None] & (slot >= begin[:, None]) & (slot < (begin + length)[:, None])
    return held.astype(jnp.float32)


def terms_kernel(sizes, *refs):
    grads, acts = refs[: len(sizes)], refs[len(sizes) : -6]
    member, query, out, held, total, sems = refs[-6:]
    block, blocks = pl.program_id(1), pl.num_programs(1)

    @pl.when((pl.program_id(0) == 0) & (block == 0))
    def _():
        copies = []
        begin = 0
        for n, (ref, size) in enumerate(zip(grads, sizes)):
            copies.append(pltpu.make_async_copy(ref, held.at[pl.ds(begin, size)], sems.at[n]))
            begin += size
        for copy in copies:
            copy.start()
        for copy in copies:
            copy.wait()

    rows = held.shape[0] * TILE
    span = min(SPAN, query.shape[2])

    @pl.when(block == 0)
    def _():
        total[...] = jnp.zeros_like(total)

    @pl.loop(0, query.shape[2] // span)
    def _(n):
        cols = pl.ds(pl.multiple_of(n * span, span), span)
        weighted = jnp.dot(
            held[...].reshape(rows, held.shape[2]),
            query[0, :, cols],
            preferred_element_type=jnp.float32,
        )
        begin = 0
        for act in acts:
            count = act.shape[0] * TILE
            act_cols = act[:, :, cols].reshape(count, span).astype(jnp.float32)
            part = weighted[begin : begin + count] * act_cols
            folded = part[:, :LANES]
            for lane in range(LANES, span, LANES):
                folded = folded + part[:, lane : lane + LANES]
            total[begin : begin + count] += folded
            begin += count

    @pl.when(block == blocks - 1)
    def _():
        out[0] = jnp.dot(
            member[...],
            total[...],
            precision=lax.Precision.HIGHEST,
            preferred_element_type=jnp.float32,
        )


def sequence_terms(grads, acts, member, query_grads):
    queries, depth, cols = query_grads.shape
    count = member.shape[0]
    width = min(cols, WIDTH)
    sizes = [g.shape[0] for g in grads]
    tiles = sum(sizes)
    rows = tiles * TILE
    arrays, blocks = [], []
    for array, at, size in acts:
        if at % size:
            array, at = array[at : at + size], 0
        arrays.append(array)
        blocks.append(
            pl.BlockSpec((size, TILE, width), lambda q, i, place=at // size: (place, 0, i))
        )
    return pl.pallas_call(
        lambda *refs: terms_kernel(sizes, *refs),
        grid=(queries, cols // width),
        in_specs=[pl.BlockSpec(memory_space=pl.ANY)] * len(sizes)
        + blocks
        + [
            pl.BlockSpec((count, rows), lambda q, i: (0, 0)),
            pl.BlockSpec((1, depth, width), lambda q, i: (q, 0, i)),
        ],
        out_specs=pl.BlockSpec((1, count, LANES), lambda q, i: (q, 0, 0)),
        out_shape=jax.ShapeDtypeStruct((queries, count, LANES), jnp.float32),
        scratch_shapes=[
            pltpu.VMEM((tiles, TILE, depth), grads[0].dtype),
            pltpu.VMEM((rows, LANES), jnp.float32),
            pltpu.SemaphoreType.DMA((len(sizes),)),
        ],
        compiler_params=pltpu.CompilerParams(vmem_limit_bytes=40 * 2**20),
        cost_estimate=pl.CostEstimate(
            flops=0,
            bytes_accessed=0,
            transcendentals=0,
        ),
        name="sequence_terms",
    )(*grads, *arrays, member, query_grads)


def after(value, *others):
    return lax.optimization_barrier((value, others))[0]


def cut(array, begin, size, axis=0):
    return lax.dynamic_slice_in_dim(array, begin, size, axis, allow_negative_indices=False)


def put(array, block, begin):
    return lax.dynamic_update_slice_in_dim(array, block, begin, 0, allow_negative_indices=False)


def local(activations, out_grads, query_grads, seq_lengths, seq_shards):
    shards = lax.axis_size("dp")
    parts = lax.axis_size("tensor")
    position = lax.axis_index("dp")
    place = lax.axis_index("tensor")
    tiles = out_grads.shape[0] // TILE
    block_cols = query_grads.shape[2]
    part_cols = block_cols // parts
    step = first = STEP if shards <= 4 else tiles
    whole = first == tiles
    routes = ([(i, i + 1) for i in range(shards - 1)], [(i + 1, i) for i in range(shards - 1)])

    grads = out_grads.reshape(tiles, TILE, out_grads.shape[1])

    act_tiles = activations.reshape(tiles, TILE, activations.shape[1])
    ids = jnp.arange(shards, dtype=jnp.int32)
    turned = position + ids
    turned = jnp.where(turned < shards, turned, turned - shards)
    begin_cols = turned * block_cols + place * part_cols
    parts_far = [cut(act_tiles, begin_cols[k], part_cols, 2) for k in range(1, shards)]
    arrived = [
        lax.ppermute(part, "dp", [(i, (i + k) % shards) for i in range(shards)])
        for k, part in enumerate(parts_far, 1)
    ]
    lead_rows = after(grads[:first], *parts_far)
    heads = [lax.ppermute(lead_rows, "dp", route) for route in routes]

    acts_own = cut(act_tiles, position * block_cols, block_cols, 2)

    count = seq_lengths.shape[0]
    order = jnp.arange(count, dtype=jnp.int32)
    same = seq_shards[:, None] == seq_shards[None, :]
    earlier = same & (order[None, :] < order[:, None])
    offset = jnp.sum(jnp.where(earlier, seq_lengths[None, :], 0), axis=1)
    member = inside(offset, seq_lengths, seq_shards == position, tiles * TILE)
    scores = sequence_terms([grads], [(acts_own, 0, tiles)], member, query_grads)

    of_shard = seq_shards[None, :] == ids[:, None]
    used = jnp.sum(jnp.where(of_shard, seq_lengths[None, :], 0), axis=1)
    filled = jnp.maximum((used + TILE - 1) // TILE, first)
    own = jnp.sum(jnp.where(ids == position, filled, 0))
    longest = jnp.maximum(jnp.sum(filled[:-1]), jnp.sum(filled[1:]))
    if lax.axis_size("groups") == 2:
        longest = jnp.maximum(longest, exchanged(longest[None], "groups", 1)[0])
    else:
        longest = lax.pmax(longest, "groups")
    nearer = (
        (ids[None, :] > ids[:, None]) & (ids[None, :] < position),
        (ids[None, :] < ids[:, None]) & (ids[None, :] > position),
    )
    bases = [jnp.sum(jnp.where(near, filled[None, :], 0), axis=1) for near in nearer]
    begins = [
        offset + TILE * jnp.sum(jnp.where(of_shard, base[:, None], 0), axis=0) for base in bases
    ]

    first_tiles = ([], [])
    for k in range(1, shards):
        for d, shard in enumerate((position - k, position + k)):
            valid = (shard >= 0) & (shard < shards)
            begin = jnp.sum(jnp.where(ids == shard, bases[d], 0))
            first_tiles[d].append(jnp.where(valid, begin, (shards - 1) * tiles))
    if not whole:
        heads = [after(head, own, longest, first_tiles, begins, scores) for head in heads]

    most = (shards - 1) * tiles
    common = first + (tiles + (shards - 3) * first) // step * step
    cuts = list(range(first, common, step)) + [common]
    last = len(cuts) - 1
    bufs = []
    if not whole:
        pads = [
            jnp.pad(after(grads, scores, *[own] * n), ((0, common), (0, 0), (0, 0))) for n in (0, 1)
        ]
        bufs = [put(buf, head, own) for buf, head in zip(pads, heads)]

    def started(bufs, at, size):
        sends = [cut(buf, at, size) for buf in bufs]
        pairs = [lax.optimization_barrier((send, buf)) for send, buf in zip(sends, bufs)]
        sends, bufs = [send for send, _ in pairs], [buf for _, buf in pairs]
        return bufs, sends, [lax.ppermute(send, "dp", route) for send, route in zip(sends, routes)]

    def stored(bufs, blocks, at):
        return [put(buf, block, own + at) for buf, block in zip(bufs, blocks)]

    def laid(blocks, d):
        buf = jnp.zeros((most + tiles, TILE, block_cols), activations.dtype)
        for block, at in zip(blocks if d == 0 else reversed(blocks), first_tiles[d]):
            buf = put(buf, block, at)
        return buf

    def terms_of(low, high, at, acts):
        size = sum(block.shape[0] for block in low)
        valid = (seq_shards < position, seq_shards > position)
        member = [inside(b - at * TILE, seq_lengths, v, size * TILE) for b, v in zip(begins, valid)]
        return sequence_terms(
            low + high, [(a, at, size) for a in acts], jnp.concatenate(member, axis=1), query_grads
        )

    low, high, low_at = [heads[0]], [heads[1]], 0
    blocks, acts, far = heads, None, scores
    for n in range(last):
        at, size = cuts[n], cuts[n + 1] - cuts[n]
        if whole:
            send = blocks
            coming = [lax.ppermute(piece, "dp", route) for piece, route in zip(send, routes)]
        else:
            bufs, send, coming = started(bufs, at, size)
        if n == 0:
            joined = jnp.concatenate([after(block, send) for block in arrived], axis=0)
            acts = gathered_cols(joined, "tensor", [send, coming])
            acts = [acts[k * tiles : (k + 1) * tiles] for k in range(shards - 1)]
            acts = [laid(acts, d) for d in (0, 1)]
        else:
            far = terms_of([after(low[0], send)] + low[1:], high, low_at, acts)
            scores = scores + far
            low, high, low_at = [], [], at
        blocks = [after(block, far) for block in coming]
        low.append(blocks[0])
        high.append(blocks[1])
        if not whole:
            bufs = stored(bufs, blocks, at)

    def ended(total, bufs, low, high, acts):
        at = common
        if total > common + first:
            bufs = [
                jnp.pad(buf[common:], ((0, total - common - first), (0, 0), (0, 0))) for buf in bufs
            ]
        else:
            bufs = [buf[common : common + total - at] for buf in bufs]
        rest = []
        while at < total:
            size = min(first, total - at)
            bufs, _, blocks = started(bufs, at - common, size)
            rest.append(([blocks[0]], [blocks[1]], at))
            if at + size < total:
                bufs = stored(bufs, blocks, at - common)
            at += size
        pieces = [(low, high, low_at)] + rest
        if total - common <= SHORT:
            pieces = [(sum((p[0] for p in pieces), []), sum((p[1] for p in pieces), []), low_at)]
        result = 0.0
        for low, high, at in pieces:
            result = result + terms_of(low, high, at, acts)
        return result

    least = tiles + (shards - 2) * first
    usual = range(least, min(common + first + step // 2, most) + 1, GRAIN)
    totals = sorted({*usual, most})
    given = (bufs, low, high, acts)
    if len(totals) == 1:
        far = ended(most, *given)
    else:
        totals = totals[::-1]
        branch = jnp.sum((longest <= jnp.array(totals[1:], jnp.int32)).astype(jnp.int32))
        far = lax.switch(
            branch, [lambda *given, total=total: ended(total, *given) for total in totals], *given
        )
    return summed(summed(jnp.sum(scores + far, axis=2), "tensor"), "dp")


def solution(mesh):
    placed = (
        P(("groups", "dp"), None),
        P(("groups", "dp"), "tensor"),
        P(None, "tensor", "dp"),
        P("groups"),
        P("groups"),
    )
    return jax.shard_map(
        local, mesh=mesh, in_specs=placed, out_specs=P(None, "groups"), check_vma=False
    )
```

```python
import jax
import jax.numpy as jnp
from jax import lax
from jax.experimental import pallas as pl
from jax.experimental.pallas import tpu as pltpu
from jax.sharding import PartitionSpec as P

LANES = 128
SPAN = 256
WIDTH = 512
TILE = 16
STEP = 12
SHORT = 0
GRAIN = 3


def exchanged(value, axis, flip):
    return lax.ppermute(value, axis, [(i, i ^ flip) for i in range(lax.axis_size(axis))])


def summed(value, axis):
    size = lax.axis_size(axis)
    if size & (size - 1):
        return lax.psum(value, axis)
    flip = 1
    while flip < size:
        value = value + exchanged(value, axis, flip)
        flip *= 2
    return value


def gathered_cols(value, axis, marks):
    size = lax.axis_size(axis)
    last = value.ndim - 1
    if size & (size - 1):
        return lax.all_gather(value, axis, axis=last, tiled=True)
    place = lax.axis_index(axis)
    blocks = [value]
    flip, n = size // 2, 0
    while flip:
        blocks[0] = after(blocks[0], marks[min(n, len(marks) - 1)])
        others = jnp.split(exchanged(jnp.concatenate(blocks, last), axis, flip), len(blocks), last)
        low = (place & flip) == 0
        blocks = [
            jnp.where(low == first, mine, other)
            for mine, other in zip(blocks, others)
            for first in (True, False)
        ]
        flip, n = flip // 2, n + 1
    return jnp.concatenate(blocks, last)


def inside(begin, length, valid, count):
    slot = jnp.arange(count, dtype=jnp.int32)[None, :]
    held = valid[:, None] & (slot >= begin[:, None]) & (slot < (begin + length)[:, None])
    return held.astype(jnp.float32)


def terms_kernel(sizes, *refs):
    grads, acts = refs[: len(sizes)], refs[len(sizes) : -6]
    member, query, out, held, total, sems = refs[-6:]
    block, blocks = pl.program_id(1), pl.num_programs(1)

    @pl.when((pl.program_id(0) == 0) & (block == 0))
    def _():
        copies = []
        begin = 0
        for n, (ref, size) in enumerate(zip(grads, sizes)):
            copies.append(pltpu.make_async_copy(ref, held.at[pl.ds(begin, size)], sems.at[n]))
            begin += size
        for copy in copies:
            copy.start()
        for copy in copies:
            copy.wait()

    rows = held.shape[0] * TILE
    span = min(SPAN, query.shape[2])

    @pl.when(block == 0)
    def _():
        total[...] = jnp.zeros_like(total)

    @pl.loop(0, query.shape[2] // span)
    def _(n):
        cols = pl.ds(pl.multiple_of(n * span, span), span)
        weighted = jnp.dot(
            held[...].reshape(rows, held.shape[2]),
            query[0, :, cols],
            preferred_element_type=jnp.float32,
        )
        begin = 0
        for act in acts:
            count = act.shape[0] * TILE
            act_cols = act[:, :, cols].reshape(count, span).astype(jnp.float32)
            part = weighted[begin : begin + count] * act_cols
            folded = part[:, :LANES]
            for lane in range(LANES, span, LANES):
                folded = folded + part[:, lane : lane + LANES]
            total[begin : begin + count] += folded
            begin += count

    @pl.when(block == blocks - 1)
    def _():
        out[0] = jnp.dot(
            member[...],
            total[...],
            precision=lax.Precision.HIGHEST,
            preferred_element_type=jnp.float32,
        )


def sequence_terms(grads, acts, member, query_grads):
    queries, depth, cols = query_grads.shape
    count = member.shape[0]
    width = min(cols, WIDTH)
    sizes = [g.shape[0] for g in grads]
    tiles = sum(sizes)
    rows = tiles * TILE
    arrays, blocks = [], []
    for array, at, size in acts:
        if at % size:
            array, at = array[at : at + size], 0
        arrays.append(array)
        blocks.append(
            pl.BlockSpec((size, TILE, width), lambda q, i, place=at // size: (place, 0, i))
        )
    return pl.pallas_call(
        lambda *refs: terms_kernel(sizes, *refs),
        grid=(queries, cols // width),
        in_specs=[pl.BlockSpec(memory_space=pl.ANY)] * len(sizes)
        + blocks
        + [
            pl.BlockSpec((count, rows), lambda q, i: (0, 0)),
            pl.BlockSpec((1, depth, width), lambda q, i: (q, 0, i)),
        ],
        out_specs=pl.BlockSpec((1, count, LANES), lambda q, i: (q, 0, 0)),
        out_shape=jax.ShapeDtypeStruct((queries, count, LANES), jnp.float32),
        scratch_shapes=[
            pltpu.VMEM((tiles, TILE, depth), grads[0].dtype),
            pltpu.VMEM((rows, LANES), jnp.float32),
            pltpu.SemaphoreType.DMA((len(sizes),)),
        ],
        compiler_params=pltpu.CompilerParams(vmem_limit_bytes=40 * 2**20),
        cost_estimate=pl.CostEstimate(
            flops=0,
            bytes_accessed=0,
            transcendentals=0,
        ),
        name="sequence_terms",
    )(*grads, *arrays, member, query_grads)


def window_kernel(at, edge, held, block, out, sem):
    size = out.shape[0]
    for i in range(size):

        @pl.when(i < edge[0])
        def _():
            pltpu.make_async_copy(held.at[at + i], out.at[i], sem).start()

        @pl.when(i >= edge[0])
        def _():
            pltpu.make_async_copy(block.at[i - edge[0]], out.at[i], sem).start()

    pltpu.make_async_copy(out, out, sem).wait()


def window(held, block, at, edge, size):
    return pl.pallas_call(
        lambda *refs: window_kernel(at, *refs),
        in_specs=[
            pl.BlockSpec(memory_space=pltpu.SMEM),
            pl.BlockSpec(memory_space=pl.ANY),
            pl.BlockSpec(memory_space=pl.ANY),
        ],
        out_specs=pl.BlockSpec(memory_space=pltpu.VMEM),
        out_shape=jax.ShapeDtypeStruct((size, *held.shape[1:]), held.dtype),
        scratch_shapes=[pltpu.SemaphoreType.DMA],
        compiler_params=pltpu.CompilerParams(vmem_limit_bytes=16 * 2**20),
        cost_estimate=pl.CostEstimate(flops=0, bytes_accessed=0, transcendentals=0),
        name="window",
    )(edge, held, block)


def after(value, *others):
    return lax.optimization_barrier((value, others))[0]


def cut(array, begin, size, axis=0):
    return lax.dynamic_slice_in_dim(array, begin, size, axis, allow_negative_indices=False)


def put(array, block, begin):
    return lax.dynamic_update_slice_in_dim(array, block, begin, 0, allow_negative_indices=False)


def local(activations, out_grads, query_grads, seq_lengths, seq_shards):
    shards = lax.axis_size("dp")
    parts = lax.axis_size("tensor")
    position = lax.axis_index("dp")
    place = lax.axis_index("tensor")
    tiles = out_grads.shape[0] // TILE
    block_cols = query_grads.shape[2]
    part_cols = block_cols // parts
    step = first = STEP if shards <= 4 else tiles
    whole = first == tiles
    routes = ([(i, i + 1) for i in range(shards - 1)], [(i + 1, i) for i in range(shards - 1)])

    grads = out_grads.reshape(tiles, TILE, out_grads.shape[1])

    act_tiles = activations.reshape(tiles, TILE, activations.shape[1])
    ids = jnp.arange(shards, dtype=jnp.int32)
    turned = position + ids
    turned = jnp.where(turned < shards, turned, turned - shards)
    begin_cols = turned * block_cols + place * part_cols
    parts_far = [cut(act_tiles, begin_cols[k], part_cols, 2) for k in range(1, shards)]
    arrived = [
        lax.ppermute(part, "dp", [(i, (i + k) % shards) for i in range(shards)])
        for k, part in enumerate(parts_far, 1)
    ]
    lead_rows = after(grads[:first], *parts_far)
    heads = [lax.ppermute(lead_rows, "dp", route) for route in routes]

    acts_own = cut(act_tiles, position * block_cols, block_cols, 2)

    count = seq_lengths.shape[0]
    order = jnp.arange(count, dtype=jnp.int32)
    same = seq_shards[:, None] == seq_shards[None, :]
    earlier = same & (order[None, :] < order[:, None])
    offset = jnp.sum(jnp.where(earlier, seq_lengths[None, :], 0), axis=1)
    member = inside(offset, seq_lengths, seq_shards == position, tiles * TILE)
    scores = sequence_terms([grads], [(acts_own, 0, tiles)], member, query_grads)

    of_shard = seq_shards[None, :] == ids[:, None]
    used = jnp.sum(jnp.where(of_shard, seq_lengths[None, :], 0), axis=1)
    filled = jnp.maximum((used + TILE - 1) // TILE, first)
    own = jnp.sum(jnp.where(ids == position, filled, 0))
    longest = jnp.maximum(jnp.sum(filled[:-1]), jnp.sum(filled[1:]))
    if lax.axis_size("groups") == 2:
        longest = jnp.maximum(longest, exchanged(longest[None], "groups", 1)[0])
    else:
        longest = lax.pmax(longest, "groups")
    nearer = (
        (ids[None, :] > ids[:, None]) & (ids[None, :] < position),
        (ids[None, :] < ids[:, None]) & (ids[None, :] > position),
    )
    bases = [jnp.sum(jnp.where(near, filled[None, :], 0), axis=1) for near in nearer]
    begins = [
        offset + TILE * jnp.sum(jnp.where(of_shard, base[:, None], 0), axis=0) for base in bases
    ]

    first_tiles = ([], [])
    for k in range(1, shards):
        for d, shard in enumerate((position - k, position + k)):
            valid = (shard >= 0) & (shard < shards)
            begin = jnp.sum(jnp.where(ids == shard, bases[d], 0))
            first_tiles[d].append(jnp.where(valid, begin, (shards - 1) * tiles))
    if not whole:
        heads = [after(head, own, longest, first_tiles, begins, scores) for head in heads]

    most = (shards - 1) * tiles
    common = first + (tiles + (shards - 3) * first) // step * step
    cuts = list(range(first, common, step)) + [common]
    last = len(cuts) - 1
    bufs = []
    if not whole:
        pads = [
            jnp.pad(after(grads, scores, *[own] * n), ((0, common), (0, 0), (0, 0))) for n in (0, 1)
        ]
        bufs, heads = lax.optimization_barrier((pads, heads))
    edge = (own - first)[None]

    def started(held, blocks, at, size):
        sends = [window(h, block, at, edge, size) for h, block in zip(held, blocks)]
        return sends, [lax.ppermute(send, "dp", route) for send, route in zip(sends, routes)]

    def stored(bufs, blocks, at):
        return [put(buf, block, own + at) for buf, block in zip(bufs, blocks)]

    def laid(blocks, d):
        buf = jnp.zeros((most + tiles, TILE, block_cols), activations.dtype)
        for block, at in zip(blocks if d == 0 else reversed(blocks), first_tiles[d]):
            buf = put(buf, block, at)
        return buf

    def terms_of(low, high, at, acts):
        size = sum(block.shape[0] for block in low)
        valid = (seq_shards < position, seq_shards > position)
        member = [inside(b - at * TILE, seq_lengths, v, size * TILE) for b, v in zip(begins, valid)]
        return sequence_terms(
            low + high, [(a, at, size) for a in acts], jnp.concatenate(member, axis=1), query_grads
        )

    low, high, low_at = [heads[0]], [heads[1]], 0
    blocks, acts, far = heads, None, scores
    for n in range(last):
        at, size = cuts[n], cuts[n + 1] - cuts[n]
        if whole:
            send = blocks
            coming = [lax.ppermute(piece, "dp", route) for piece, route in zip(send, routes)]
        else:
            send, coming = started(bufs if n else (grads, grads), blocks, at, size)
            bufs = [after(buf, piece) for buf, piece in zip(bufs, send)]
            bufs = stored(bufs, blocks, cuts[n - 1] if n else 0)
        if n == 0:
            joined = jnp.concatenate([after(block, heads) for block in arrived], axis=0)
            acts = gathered_cols(joined, "tensor", [heads, send])
            acts = [acts[k * tiles : (k + 1) * tiles] for k in range(shards - 1)]
            acts = [laid(acts, d) for d in (0, 1)]
        else:
            far = terms_of([after(low[0], send)] + low[1:], high, low_at, acts)
            scores = scores + far
            low, high, low_at = [], [], at
        blocks = [after(block, far) for block in coming]
        low.append(blocks[0])
        high.append(blocks[1])

    def ended(total, bufs, low, high, acts):
        at = common
        blocks = [low[-1], high[-1]]
        rest = []
        while at < total:
            size = min(step, total - at)
            send, coming = started(bufs, blocks, at, size)
            if at + size < total:
                bufs = [after(buf, piece) for buf, piece in zip(bufs, send)]
                if bufs[0].shape[0] < tiles + total - step:
                    more = tiles + total - step - bufs[0].shape[0]
                    bufs = [jnp.pad(buf, ((0, more), (0, 0), (0, 0))) for buf in bufs]
                bufs = stored(bufs, blocks, at - step)
            blocks = coming
            rest.append(([blocks[0]], [blocks[1]], at))
            at += size
        pieces = [(low, high, low_at)] + rest
        if total - common <= SHORT:
            pieces = [(sum((p[0] for p in pieces), []), sum((p[1] for p in pieces), []), low_at)]
        result = 0.0
        for low, high, at in pieces:
            result = result + terms_of(low, high, at, acts)
        return result

    least = tiles + (shards - 2) * first
    usual = range(least, min(common + first + step // 2, most) + 1, GRAIN)
    totals = sorted({*usual, most})
    given = (bufs, low, high, acts)
    if len(totals) == 1:
        far = ended(most, *given)
    else:
        totals = totals[::-1]
        branch = jnp.sum((longest <= jnp.array(totals[1:], jnp.int32)).astype(jnp.int32))
        far = lax.switch(
            branch, [lambda *given, total=total: ended(total, *given) for total in totals], *given
        )
    return summed(summed(jnp.sum(scores + far, axis=2), "tensor"), "dp")


def solution(mesh):
    placed = (
        P(("groups", "dp"), None),
        P(("groups", "dp"), "tensor"),
        P(None, "tensor", "dp"),
        P("groups"),
        P("groups"),
    )
    return jax.shard_map(
        local, mesh=mesh, in_specs=placed, out_specs=P(None, "groups"), check_vma=False
    )
```

```python
import jax
import jax.numpy as jnp
from jax import lax
from jax.experimental import pallas as pl
from jax.experimental.pallas import tpu as pltpu
from jax.sharding import PartitionSpec as P

LANES = 128
SPAN = 256
WIDTH = 512
TILE = 16
STEP = 12
GRAIN = 3


def exchanged(value, axis, flip):
    return lax.ppermute(value, axis, [(i, i ^ flip) for i in range(lax.axis_size(axis))])


def summed(value, axis):
    size = lax.axis_size(axis)
    if size & (size - 1):
        return lax.psum(value, axis)
    flip = 1
    while flip < size:
        value = value + exchanged(value, axis, flip)
        flip *= 2
    return value


def gathered_cols(value, axis, marks):
    size = lax.axis_size(axis)
    last = value.ndim - 1
    if size & (size - 1):
        return lax.all_gather(value, axis, axis=last, tiled=True)
    place = lax.axis_index(axis)
    blocks = [value]
    flip, n = size // 2, 0
    while flip:
        blocks[0] = after(blocks[0], marks[min(n, len(marks) - 1)])
        others = jnp.split(exchanged(jnp.concatenate(blocks, last), axis, flip), len(blocks), last)
        low = (place & flip) == 0
        blocks = [
            jnp.where(low == first, mine, other)
            for mine, other in zip(blocks, others)
            for first in (True, False)
        ]
        flip, n = flip // 2, n + 1
    return jnp.concatenate(blocks, last)


def inside(begin, length, valid, count):
    slot = jnp.arange(count, dtype=jnp.int32)[None, :]
    held = valid[:, None] & (slot >= begin[:, None]) & (slot < (begin + length)[:, None])
    return held.astype(jnp.float32)


def terms_kernel(sizes, *refs):
    grads, acts = refs[: len(sizes)], refs[len(sizes) : -6]
    member, query, out, held, total, sems = refs[-6:]
    block, blocks = pl.program_id(1), pl.num_programs(1)

    @pl.when((pl.program_id(0) == 0) & (block == 0))
    def _():
        copies = []
        begin = 0
        for n, (ref, size) in enumerate(zip(grads, sizes)):
            copies.append(pltpu.make_async_copy(ref, held.at[pl.ds(begin, size)], sems.at[n]))
            begin += size
        for copy in copies:
            copy.start()
        for copy in copies:
            copy.wait()

    rows = held.shape[0] * TILE
    span = min(SPAN, query.shape[2])

    @pl.when(block == 0)
    def _():
        total[...] = jnp.zeros_like(total)

    @pl.loop(0, query.shape[2] // span)
    def _(n):
        cols = pl.ds(pl.multiple_of(n * span, span), span)
        weighted = jnp.dot(
            held[...].reshape(rows, held.shape[2]),
            query[0, :, cols],
            preferred_element_type=jnp.float32,
        )
        begin = 0
        for act in acts:
            count = act.shape[0] * TILE
            act_cols = act[:, :, cols].reshape(count, span).astype(jnp.float32)
            part = weighted[begin : begin + count] * act_cols
            folded = part[:, :LANES]
            for lane in range(LANES, span, LANES):
                folded = folded + part[:, lane : lane + LANES]
            total[begin : begin + count] += folded
            begin += count

    @pl.when(block == blocks - 1)
    def _():
        out[0] = jnp.dot(
            member[...],
            total[...],
            precision=lax.Precision.HIGHEST,
            preferred_element_type=jnp.float32,
        )


def sequence_terms(grads, acts, member, query_grads):
    queries, depth, cols = query_grads.shape
    count = member.shape[0]
    width = min(cols, WIDTH)
    sizes = [g.shape[0] for g in grads]
    tiles = sum(sizes)
    rows = tiles * TILE
    arrays, blocks = [], []
    for array, at, size in acts:
        if at % size:
            array, at = array[at : at + size], 0
        arrays.append(array)
        blocks.append(
            pl.BlockSpec((size, TILE, width), lambda q, i, place=at // size: (place, 0, i))
        )
    return pl.pallas_call(
        lambda *refs: terms_kernel(sizes, *refs),
        grid=(queries, cols // width),
        in_specs=[pl.BlockSpec(memory_space=pl.ANY)] * len(sizes)
        + blocks
        + [
            pl.BlockSpec((count, rows), lambda q, i: (0, 0)),
            pl.BlockSpec((1, depth, width), lambda q, i: (q, 0, i)),
        ],
        out_specs=pl.BlockSpec((1, count, LANES), lambda q, i: (q, 0, 0)),
        out_shape=jax.ShapeDtypeStruct((queries, count, LANES), jnp.float32),
        scratch_shapes=[
            pltpu.VMEM((tiles, TILE, depth), grads[0].dtype),
            pltpu.VMEM((rows, LANES), jnp.float32),
            pltpu.SemaphoreType.DMA((len(sizes),)),
        ],
        compiler_params=pltpu.CompilerParams(vmem_limit_bytes=40 * 2**20),
        cost_estimate=pl.CostEstimate(
            flops=0,
            bytes_accessed=0,
            transcendentals=0,
        ),
        name="sequence_terms",
    )(*grads, *arrays, member, query_grads)


def window_kernel(at, edge, held, block, out, sem):
    size = out.shape[0]
    for i in range(size):

        @pl.when(i < edge[0])
        def _():
            pltpu.make_async_copy(held.at[at + i], out.at[i], sem).start()

        @pl.when(i >= edge[0])
        def _():
            pltpu.make_async_copy(block.at[i - edge[0]], out.at[i], sem).start()

    pltpu.make_async_copy(out, out, sem).wait()


def window(held, block, at, edge, size):
    return pl.pallas_call(
        lambda *refs: window_kernel(at, *refs),
        in_specs=[
            pl.BlockSpec(memory_space=pltpu.SMEM),
            pl.BlockSpec(memory_space=pl.ANY),
            pl.BlockSpec(memory_space=pl.ANY),
        ],
        out_specs=pl.BlockSpec(memory_space=pltpu.VMEM),
        out_shape=jax.ShapeDtypeStruct((size, *held.shape[1:]), held.dtype),
        scratch_shapes=[pltpu.SemaphoreType.DMA],
        compiler_params=pltpu.CompilerParams(vmem_limit_bytes=16 * 2**20),
        cost_estimate=pl.CostEstimate(flops=0, bytes_accessed=0, transcendentals=0),
        name="window",
    )(edge, held, block)


def after(value, *others):
    return lax.optimization_barrier((value, others))[0]


def cut(array, begin, size, axis=0):
    return lax.dynamic_slice_in_dim(array, begin, size, axis, allow_negative_indices=False)


def put(array, block, begin):
    return lax.dynamic_update_slice_in_dim(array, block, begin, 0, allow_negative_indices=False)


def local(activations, out_grads, query_grads, seq_lengths, seq_shards):
    shards = lax.axis_size("dp")
    parts = lax.axis_size("tensor")
    position = lax.axis_index("dp")
    place = lax.axis_index("tensor")
    tiles = out_grads.shape[0] // TILE
    block_cols = query_grads.shape[2]
    part_cols = block_cols // parts
    step = first = STEP if shards <= 4 else tiles
    whole = first == tiles
    routes = ([(i, i + 1) for i in range(shards - 1)], [(i + 1, i) for i in range(shards - 1)])

    grads = out_grads.reshape(tiles, TILE, out_grads.shape[1])

    act_tiles = activations.reshape(tiles, TILE, activations.shape[1])
    ids = jnp.arange(shards, dtype=jnp.int32)
    turned = position + ids
    turned = jnp.where(turned < shards, turned, turned - shards)
    begin_cols = turned * block_cols + place * part_cols
    lead_rows = grads[:first]
    heads = [lax.ppermute(lead_rows, "dp", route) for route in routes]
    parts_far = [after(cut(act_tiles, begin_cols[k], part_cols, 2), lead_rows) for k in range(1, shards)]
    arrived = [
        lax.ppermute(part, "dp", [(i, (i + k) % shards) for i in range(shards)])
        for k, part in enumerate(parts_far, 1)
    ]

    acts_own = cut(act_tiles, position * block_cols, block_cols, 2)

    count = seq_lengths.shape[0]
    order = jnp.arange(count, dtype=jnp.int32)
    same = seq_shards[:, None] == seq_shards[None, :]
    earlier = same & (order[None, :] < order[:, None])
    offset = jnp.sum(jnp.where(earlier, seq_lengths[None, :], 0), axis=1)
    member = inside(offset, seq_lengths, seq_shards == position, tiles * TILE)
    scores = sequence_terms([grads], [(acts_own, 0, tiles)], member, query_grads)

    of_shard = seq_shards[None, :] == ids[:, None]
    used = jnp.sum(jnp.where(of_shard, seq_lengths[None, :], 0), axis=1)
    filled = jnp.maximum((used + TILE - 1) // TILE, first)
    own = jnp.sum(jnp.where(ids == position, filled, 0))
    longest = jnp.maximum(jnp.sum(filled[:-1]), jnp.sum(filled[1:]))
    if lax.axis_size("groups") == 2:
        longest = jnp.maximum(longest, exchanged(longest[None], "groups", 1)[0])
    else:
        longest = lax.pmax(longest, "groups")
    nearer = (
        (ids[None, :] > ids[:, None]) & (ids[None, :] < position),
        (ids[None, :] < ids[:, None]) & (ids[None, :] > position),
    )
    bases = [jnp.sum(jnp.where(near, filled[None, :], 0), axis=1) for near in nearer]
    begins = [
        offset + TILE * jnp.sum(jnp.where(of_shard, base[:, None], 0), axis=0) for base in bases
    ]

    first_tiles = ([], [])
    for k in range(1, shards):
        for d, shard in enumerate((position - k, position + k)):
            valid = (shard >= 0) & (shard < shards)
            begin = jnp.sum(jnp.where(ids == shard, bases[d], 0))
            first_tiles[d].append(jnp.where(valid, begin, (shards - 1) * tiles))
    if not whole:
        heads = [after(head, own, longest, first_tiles, begins, scores) for head in heads]

    most = (shards - 1) * tiles
    common = first + (tiles + (shards - 3) * first) // step * step
    cuts = list(range(first, common, step)) + [common]
    last = len(cuts) - 1
    bufs = []
    if not whole:
        pads = [
            jnp.pad(after(grads, scores, *[own] * n), ((0, common), (0, 0), (0, 0))) for n in (0, 1)
        ]
        bufs, heads = lax.optimization_barrier((pads, heads))
    edge = (own - first)[None]

    def started(held, blocks, at, size):
        sends = [window(h, block, at, edge, size) for h, block in zip(held, blocks)]
        return sends, [lax.ppermute(send, "dp", route) for send, route in zip(sends, routes)]

    def stored(bufs, blocks, at):
        return [put(buf, block, own + at) for buf, block in zip(bufs, blocks)]

    def laid(blocks, d):
        buf = jnp.zeros((most + tiles, TILE, block_cols), activations.dtype)
        for block, at in zip(blocks if d == 0 else reversed(blocks), first_tiles[d]):
            buf = put(buf, block, at)
        return buf

    def terms_of(low, high, at, acts):
        size = sum(block.shape[0] for block in low)
        valid = (seq_shards < position, seq_shards > position)
        member = [inside(b - at * TILE, seq_lengths, v, size * TILE) for b, v in zip(begins, valid)]
        return sequence_terms(
            low + high, [(a, at, size) for a in acts], jnp.concatenate(member, axis=1), query_grads
        )

    low, high, low_at = [heads[0]], [heads[1]], 0
    blocks, acts, far = heads, None, scores
    for n in range(last):
        at, size = cuts[n], cuts[n + 1] - cuts[n]
        if whole:
            send = blocks
            coming = [lax.ppermute(piece, "dp", route) for piece, route in zip(send, routes)]
        else:
            send, coming = started(bufs if n else (grads, grads), blocks, at, size)
            bufs = [after(buf, piece) for buf, piece in zip(bufs, send)]
            bufs = stored(bufs, blocks, cuts[n - 1] if n else 0)
        if n == 0:
            joined = jnp.concatenate([after(block, send) for block in arrived], axis=0)
            acts = gathered_cols(joined, "tensor", [send])
            acts = [acts[k * tiles : (k + 1) * tiles] for k in range(shards - 1)]
            acts = [laid(acts, d) for d in (0, 1)]
        else:
            far = terms_of([after(low[0], send)] + low[1:], high, low_at, acts)
            scores = scores + far
            low, high, low_at = [], [], at
        blocks = [after(block, far) for block in coming]
        low.append(blocks[0])
        high.append(blocks[1])

    def ended(total, bufs, low, high, acts):
        at = common
        blocks = [low[-1], high[-1]]
        rest = []
        while at < total:
            size = min(step, total - at)
            send, coming = started(bufs, blocks, at, size)
            if at + size < total:
                bufs = [after(buf, piece) for buf, piece in zip(bufs, send)]
                more = tiles + at - bufs[0].shape[0]
                if more > 0:
                    bufs = [jnp.pad(buf, ((0, more), (0, 0), (0, 0))) for buf in bufs]
                bufs = stored(bufs, blocks, at - step)
            blocks = coming
            rest.append(([blocks[0]], [blocks[1]], at))
            at += size
        pieces = [(low, high, low_at)] + rest
        result = 0.0
        for low, high, at in pieces:
            result = result + terms_of(low, high, at, acts)
        return result

    least = tiles + (shards - 2) * first
    usual = range(least, min(common + first + step // 2, most) + 1, GRAIN)
    totals = sorted({*usual, min(common + 2 * first, most), most})
    given = (bufs, low, high, acts)
    if len(totals) == 1:
        far = ended(most, *given)
    else:
        totals = totals[::-1]
        branch = jnp.sum((longest <= jnp.array(totals[1:], jnp.int32)).astype(jnp.int32))
        far = lax.switch(
            branch, [lambda *given, total=total: ended(total, *given) for total in totals], *given
        )
    return summed(summed(jnp.sum(scores + far, axis=2), "tensor"), "dp")


def solution(mesh):
    placed = (
        P(("groups", "dp"), None),
        P(("groups", "dp"), "tensor"),
        P(None, "tensor", "dp"),
        P("groups"),
        P("groups"),
    )
    return jax.shard_map(
        local, mesh=mesh, in_specs=placed, out_specs=P(None, "groups"), check_vma=False
    )
```

```python
import jax
import jax.numpy as jnp
from jax import lax
from jax.experimental import pallas as pl
from jax.experimental.pallas import tpu as pltpu
from jax.sharding import PartitionSpec as P

LANES = 128
SPAN = 256
WIDTH = 512
TILE = 16
STEP = 12
GRAIN = 3


def exchanged(value, axis, flip):
    return lax.ppermute(value, axis, [(i, i ^ flip) for i in range(lax.axis_size(axis))])


def summed(value, axis):
    size = lax.axis_size(axis)
    if size & (size - 1):
        return lax.psum(value, axis)
    flip = 1
    while flip < size:
        value = value + exchanged(value, axis, flip)
        flip *= 2
    return value


def gathered_cols(value, axis, marks):
    size = lax.axis_size(axis)
    last = value.ndim - 1
    if size & (size - 1):
        return lax.all_gather(value, axis, axis=last, tiled=True)
    place = lax.axis_index(axis)
    blocks = [value]
    flip, n = size // 2, 0
    while flip:
        blocks[0] = after(blocks[0], marks[min(n, len(marks) - 1)])
        others = jnp.split(exchanged(jnp.concatenate(blocks, last), axis, flip), len(blocks), last)
        low = (place & flip) == 0
        blocks = [
            jnp.where(low == first, mine, other)
            for mine, other in zip(blocks, others)
            for first in (True, False)
        ]
        flip, n = flip // 2, n + 1
    return jnp.concatenate(blocks, last)


def inside(begin, length, valid, count):
    slot = jnp.arange(count, dtype=jnp.int32)[None, :]
    held = valid[:, None] & (slot >= begin[:, None]) & (slot < (begin + length)[:, None])
    return held.astype(jnp.float32)


def terms_kernel(sizes, *refs):
    grads, acts = refs[: len(sizes)], refs[len(sizes) : -6]
    member, query, out, held, total, sems = refs[-6:]
    block, blocks = pl.program_id(1), pl.num_programs(1)

    @pl.when((pl.program_id(0) == 0) & (block == 0))
    def _():
        copies = []
        begin = 0
        for n, (ref, size) in enumerate(zip(grads, sizes)):
            copies.append(pltpu.make_async_copy(ref, held.at[pl.ds(begin, size)], sems.at[n]))
            begin += size
        for copy in copies:
            copy.start()
        for copy in copies:
            copy.wait()

    rows = held.shape[0] * TILE
    span = min(SPAN, query.shape[2])

    @pl.when(block == 0)
    def _():
        total[...] = jnp.zeros_like(total)

    @pl.loop(0, query.shape[2] // span)
    def _(n):
        cols = pl.ds(pl.multiple_of(n * span, span), span)
        weighted = jnp.dot(
            held[...].reshape(rows, held.shape[2]),
            query[0, :, cols],
            preferred_element_type=jnp.float32,
        )
        begin = 0
        for act in acts:
            count = act.shape[0] * TILE
            act_cols = act[:, :, cols].reshape(count, span).astype(jnp.float32)
            part = weighted[begin : begin + count] * act_cols
            folded = part[:, :LANES]
            for lane in range(LANES, span, LANES):
                folded = folded + part[:, lane : lane + LANES]
            total[begin : begin + count] += folded
            begin += count

    @pl.when(block == blocks - 1)
    def _():
        out[0] = jnp.dot(
            member[...],
            total[...],
            precision=lax.Precision.HIGHEST,
            preferred_element_type=jnp.float32,
        )


def sequence_terms(grads, acts, member, query_grads):
    queries, depth, cols = query_grads.shape
    count = member.shape[0]
    width = min(cols, WIDTH)
    sizes = [g.shape[0] for g in grads]
    tiles = sum(sizes)
    rows = tiles * TILE
    arrays, blocks = [], []
    for array, at, size in acts:
        if at % size:
            array, at = array[at : at + size], 0
        arrays.append(array)
        blocks.append(
            pl.BlockSpec((size, TILE, width), lambda q, i, place=at // size: (place, 0, i))
        )
    return pl.pallas_call(
        lambda *refs: terms_kernel(sizes, *refs),
        grid=(queries, cols // width),
        in_specs=[pl.BlockSpec(memory_space=pl.ANY)] * len(sizes)
        + blocks
        + [
            pl.BlockSpec((count, rows), lambda q, i: (0, 0)),
            pl.BlockSpec((1, depth, width), lambda q, i: (q, 0, i)),
        ],
        out_specs=pl.BlockSpec((1, count, LANES), lambda q, i: (q, 0, 0)),
        out_shape=jax.ShapeDtypeStruct((queries, count, LANES), jnp.float32),
        scratch_shapes=[
            pltpu.VMEM((tiles, TILE, depth), grads[0].dtype),
            pltpu.VMEM((rows, LANES), jnp.float32),
            pltpu.SemaphoreType.DMA((len(sizes),)),
        ],
        compiler_params=pltpu.CompilerParams(vmem_limit_bytes=40 * 2**20),
        cost_estimate=pl.CostEstimate(
            flops=0,
            bytes_accessed=0,
            transcendentals=0,
        ),
        name="sequence_terms",
    )(*grads, *arrays, member, query_grads)


def window_kernel(at, edge, held, block, out, sem):
    size = out.shape[0]
    for i in range(size):

        @pl.when(i < edge[0])
        def _():
            pltpu.make_async_copy(held.at[at + i], out.at[i], sem).start()

        @pl.when(i >= edge[0])
        def _():
            pltpu.make_async_copy(block.at[i - edge[0]], out.at[i], sem).start()

    pltpu.make_async_copy(out, out, sem).wait()


def window(held, block, at, edge, size):
    return pl.pallas_call(
        lambda *refs: window_kernel(at, *refs),
        in_specs=[
            pl.BlockSpec(memory_space=pltpu.SMEM),
            pl.BlockSpec(memory_space=pl.ANY),
            pl.BlockSpec(memory_space=pl.ANY),
        ],
        out_specs=pl.BlockSpec(memory_space=pltpu.VMEM),
        out_shape=jax.ShapeDtypeStruct((size, *held.shape[1:]), held.dtype),
        scratch_shapes=[pltpu.SemaphoreType.DMA],
        compiler_params=pltpu.CompilerParams(vmem_limit_bytes=16 * 2**20),
        cost_estimate=pl.CostEstimate(flops=0, bytes_accessed=0, transcendentals=0),
        name="window",
    )(edge, held, block)


def after(value, *others):
    return lax.optimization_barrier((value, others))[0]


def cut(array, begin, size, axis=0):
    return lax.dynamic_slice_in_dim(array, begin, size, axis, allow_negative_indices=False)


def put(array, block, begin):
    return lax.dynamic_update_slice_in_dim(array, block, begin, 0, allow_negative_indices=False)


def local(activations, out_grads, query_grads, seq_lengths, seq_shards):
    shards = lax.axis_size("dp")
    parts = lax.axis_size("tensor")
    position = lax.axis_index("dp")
    place = lax.axis_index("tensor")
    tiles = out_grads.shape[0] // TILE
    block_cols = query_grads.shape[2]
    part_cols = block_cols // parts
    step = first = STEP if shards <= 4 else tiles
    whole = first == tiles
    routes = ([(i, i + 1) for i in range(shards - 1)], [(i + 1, i) for i in range(shards - 1)])

    grads = out_grads.reshape(tiles, TILE, out_grads.shape[1])

    act_tiles = activations.reshape(tiles, TILE, activations.shape[1])
    ids = jnp.arange(shards, dtype=jnp.int32)
    turned = position + ids
    turned = jnp.where(turned < shards, turned, turned - shards)
    begin_cols = turned * block_cols + place * part_cols
    lead_rows = grads[:first]
    heads = [lax.ppermute(lead_rows, "dp", route) for route in routes]
    parts_far = [after(cut(act_tiles, begin_cols[k], part_cols, 2), lead_rows) for k in range(1, shards)]
    arrived = [
        lax.ppermute(part, "dp", [(i, (i + k) % shards) for i in range(shards)])
        for k, part in enumerate(parts_far, 1)
    ]

    acts_own = cut(act_tiles, position * block_cols, block_cols, 2)

    count = seq_lengths.shape[0]
    order = jnp.arange(count, dtype=jnp.int32)
    same = seq_shards[:, None] == seq_shards[None, :]
    earlier = same & (order[None, :] < order[:, None])
    offset = jnp.sum(jnp.where(earlier, seq_lengths[None, :], 0), axis=1)
    member = inside(offset, seq_lengths, seq_shards == position, tiles * TILE)
    scores = sequence_terms([grads], [(acts_own, 0, tiles)], member, query_grads)

    of_shard = seq_shards[None, :] == ids[:, None]
    used = jnp.sum(jnp.where(of_shard, seq_lengths[None, :], 0), axis=1)
    filled = jnp.maximum((used + TILE - 1) // TILE, first)
    own = jnp.sum(jnp.where(ids == position, filled, 0))
    longest = jnp.maximum(jnp.sum(filled[:-1]), jnp.sum(filled[1:]))
    if lax.axis_size("groups") == 2:
        longest = jnp.maximum(longest, exchanged(longest[None], "groups", 1)[0])
    else:
        longest = lax.pmax(longest, "groups")
    nearer = (
        (ids[None, :] > ids[:, None]) & (ids[None, :] < position),
        (ids[None, :] < ids[:, None]) & (ids[None, :] > position),
    )
    bases = [jnp.sum(jnp.where(near, filled[None, :], 0), axis=1) for near in nearer]
    begins = [
        offset + TILE * jnp.sum(jnp.where(of_shard, base[:, None], 0), axis=0) for base in bases
    ]

    first_tiles = ([], [])
    for k in range(1, shards):
        for d, shard in enumerate((position - k, position + k)):
            valid = (shard >= 0) & (shard < shards)
            begin = jnp.sum(jnp.where(ids == shard, bases[d], 0))
            first_tiles[d].append(jnp.where(valid, begin, (shards - 1) * tiles))
    if not whole:
        heads = [after(head, own, longest, first_tiles, begins, scores) for head in heads]

    most = (shards - 1) * tiles
    common = first + (tiles + (shards - 3) * first) // step * step
    cuts = list(range(first, common, step)) + [common]
    last = len(cuts) - 1
    bufs = []
    if not whole:
        pads = [
            jnp.pad(after(grads, scores, *[own] * n), ((0, common), (0, 0), (0, 0))) for n in (0, 1)
        ]
        bufs, heads = lax.optimization_barrier((pads, heads))
    edge = (own - first)[None]

    def started(held, blocks, at, size):
        sends = []
        for h, block in zip(held, blocks):
            sends.append(window(h, after(block, sends), at, edge, size))
        return sends, [lax.ppermute(send, "dp", route) for send, route in zip(sends, routes)]

    def stored(bufs, blocks, at):
        return [put(buf, block, own + at) for buf, block in zip(bufs, blocks)]

    def laid(blocks, d):
        buf = jnp.zeros((most + tiles, TILE, block_cols), activations.dtype)
        for block, at in zip(blocks if d == 0 else reversed(blocks), first_tiles[d]):
            buf = put(buf, block, at)
        return buf

    def terms_of(low, high, at, acts):
        size = sum(block.shape[0] for block in low)
        valid = (seq_shards < position, seq_shards > position)
        member = [inside(b - at * TILE, seq_lengths, v, size * TILE) for b, v in zip(begins, valid)]
        return sequence_terms(
            low + high, [(a, at, size) for a in acts], jnp.concatenate(member, axis=1), query_grads
        )

    low, high, low_at = [heads[0]], [heads[1]], 0
    blocks, acts, far = heads, None, scores
    for n in range(last):
        at, size = cuts[n], cuts[n + 1] - cuts[n]
        if whole:
            send = blocks
            coming = [lax.ppermute(piece, "dp", route) for piece, route in zip(send, routes)]
        else:
            send, coming = started(bufs if n else (grads, grads), blocks, at, size)
            bufs = [after(buf, piece) for buf, piece in zip(bufs, send)]
            bufs = stored(bufs, blocks, cuts[n - 1] if n else 0)
        if n == 0:
            joined = jnp.concatenate([after(block, send) for block in arrived], axis=0)
            acts = gathered_cols(joined, "tensor", [send])
            acts = [acts[k * tiles : (k + 1) * tiles] for k in range(shards - 1)]
            acts = [laid(acts, d) for d in (0, 1)]
        else:
            far = terms_of([after(low[0], send)] + low[1:], high, low_at, acts)
            scores = scores + far
            low, high, low_at = [], [], at
        blocks = [after(block, far) for block in coming]
        low.append(blocks[0])
        high.append(blocks[1])

    def ended(total, bufs, low, high, acts):
        at = common
        blocks = [low[-1], high[-1]]
        rest = []
        while at < total:
            size = min(step, total - at)
            send, coming = started(bufs, blocks, at, size)
            if at + size < total:
                bufs = [after(buf, piece) for buf, piece in zip(bufs, send)]
                more = tiles + at - bufs[0].shape[0]
                if more > 0:
                    bufs = [jnp.pad(buf, ((0, more), (0, 0), (0, 0))) for buf in bufs]
                bufs = stored(bufs, blocks, at - step)
            blocks = coming
            rest.append(([blocks[0]], [blocks[1]], at))
            at += size
        pieces = [(low, high, low_at)] + rest
        result = 0.0
        for low, high, at in pieces:
            result = result + terms_of(low, high, at, acts)
        return result

    least = tiles + (shards - 2) * first
    usual = range(least, min(common + first + step // 2, most) + 1, GRAIN)
    totals = sorted({*usual, min(common + 2 * first, most), most})
    given = (bufs, low, high, acts)
    if len(totals) == 1:
        far = ended(most, *given)
    else:
        totals = totals[::-1]
        branch = jnp.sum((longest <= jnp.array(totals[1:], jnp.int32)).astype(jnp.int32))
        far = lax.switch(
            branch, [lambda *given, total=total: ended(total, *given) for total in totals], *given
        )
    return summed(summed(jnp.sum(scores + far, axis=2), "tensor"), "dp")


def solution(mesh):
    placed = (
        P(("groups", "dp"), None),
        P(("groups", "dp"), "tensor"),
        P(None, "tensor", "dp"),
        P("groups"),
        P("groups"),
    )
    return jax.shard_map(
        local, mesh=mesh, in_specs=placed, out_specs=P(None, "groups"), check_vma=False
    )
```
